32 devices in a mesh: seq: 4 (over z), exp: 8 (over y, x, core).
Axes of the slice: x: 2, y: 2, z: 4, core: 2. Of those that a mesh axis runs over, the one named last changes fastest.
Arguments:
- tokens: bfloat16 [6144, 2048], P(('seq', 'exp')), may hold values from -1500 to 1500
- norm_gain: float32 [2048], replicated, may hold values from 0.1 to 1.9
- norm_bias: float32 [2048], replicated, may hold values from -3 to 3
- routes: int32 [6144, 6], P(('seq', 'exp')), may hold values from 0 to 7, as said below
- gate_codes: int32 [6144, 6], P(('seq', 'exp')), may hold values from 1 to 1023
- w_in: bfloat16 [8, 2048, 1408], P('exp'), may hold values from -0.125 to 0.125
- w_out: bfloat16 [8, 704, 2048], P('exp'), may hold values from -0.21875 to 0.21875
Outputs:
- mixed: bfloat16 [6144, 2048], P(('seq', 'exp'))
The draws below stay inside these ranges and needn't reach their ends.
Inputs may be any that keep to these rules, and one draw needn't show every extreme that they name: `routes`: each row names 6 different experts; in the rows of every device one and the same expert is named exactly 192 times, more often than any other; every other expert is named at most 182 times there; one expert other than it is named exactly 182 times by the rows of every device.
All inputs are finite; a program needn't handle non-finite values.
Results may differ from the reference program's by a relative error of at most 0.0071.
Values may be sent and summed in bfloat16 or wider, within the bound.
A program may use at most 128 MiB of HBM per device.

```python
import math
import jax
import jax.numpy as jnp
from jax import lax

D = 2048
FF = 704
TOP = 6
TOK_DEV = 192
EXPERTS = 8
TOKENS = 6144
CAP = 162
HOTMAX = 192
OVER = 182


def pick_pair(key):
    hot_expert = jax.random.randint(key, (), 0, EXPERTS - 1, dtype=jnp.int32)
    offset = jax.random.randint(jax.random.fold_in(key, 1), (), 1, EXPERTS, dtype=jnp.int32)
    full_expert = hot_expert + 1 + offset % (EXPERTS - 1 - hot_expert)
    return (hot_expert, full_expert.astype(jnp.int32))


def block_routes(key, hot_expert, full_expert):
    pair_key, order_key, row_key, column_key = jax.random.split(key, 4)
    others = EXPERTS - 2
    remaining = TOK_DEV * TOP - HOTMAX - OVER
    base_load = remaining // others
    leftover = remaining % others
    half_range = max(min(OVER - base_load - 1, base_load), 0)
    pair_count = others // 2
    position = jnp.arange(others, dtype=jnp.int32)
    other_load = base_load + (position < leftover).astype(jnp.int32)
    shift_sizes = jax.random.randint(pair_key, (pair_count,), 0, half_range + 1, dtype=jnp.int32)
    changes = jnp.zeros((others,), jnp.int32)
    changes = changes.at[0:2 * pair_count:2].add(shift_sizes).at[1:2 * pair_count:2].add(-shift_sizes)
    other_load = (other_load + changes).astype(jnp.int32)
    ordering = jax.random.permutation(order_key, EXPERTS).astype(jnp.int32)
    sort_key = jnp.where(ordering == hot_expert, -2, jnp.where(ordering == full_expert, -1, jnp.arange(EXPERTS, dtype=jnp.int32)))
    listing = ordering[jnp.argsort(sort_key)]
    run_lengths = jnp.concatenate([jnp.array([HOTMAX, OVER], jnp.int32), other_load])
    run_ends = jnp.cumsum(run_lengths).astype(jnp.int32)
    slot_index = jnp.arange(TOK_DEV * TOP, dtype=jnp.int32)
    run_index = jnp.sum((slot_index[:, None] >= run_ends[None, :]).astype(jnp.int32), axis=1).astype(jnp.int32)
    expert_ids = listing[run_index]
    table_ids = expert_ids.reshape(TOP, TOK_DEV).T
    table_ids = table_ids[jax.random.permutation(row_key, TOK_DEV)]
    column_keys = jax.random.split(column_key, TOK_DEV)
    table_ids = jax.vmap(jax.random.permutation)(column_keys, table_ids)
    return table_ids.astype(jnp.int32)


def draw_routes(key, part):
    hot_expert, full_expert = pick_pair(key)
    key = jax.random.fold_in(key, 5)
    block_keys = jax.random.split(key, TOKENS // TOK_DEV)

    def one_block(block_key):
        return block_routes(block_key, hot_expert, full_expert)
    return jax.vmap(one_block)(block_keys).reshape(TOKENS, TOP).astype(jnp.int32)


def draw_tokens(key, part):
    key = jax.random.fold_in(key, 7)
    value_key, row_key, column_key = jax.random.split(key, 3)
    row_scale = jnp.exp(jax.random.uniform(row_key, (TOKENS, 1), jnp.float32, 0.0, math.log(10.0)))
    column_scale = jnp.exp(jax.random.uniform(column_key, (1, D), jnp.float32, 0.0, math.log(10.0)))
    values = jnp.clip(jax.random.normal(value_key, (TOKENS, D), jnp.float32), -5.0, 5.0)
    return (values * row_scale * column_scale).astype(jnp.bfloat16)


def with_ends(values, rng, least, top_value):
    index_at = [jax.random.randint(jax.random.fold_in(rng, axis), (), 0, length) for axis, length in enumerate(values.shape)]
    widest = values.shape.index(max(values.shape))
    neighbour = index_at[:widest] + [(index_at[widest] + 1) % values.shape[widest]] + index_at[widest + 1:]
    return values.at[tuple(index_at)].set(least).at[tuple(neighbour)].set(top_value)


def level_of(rng, extent, pieces, smallest, largest):
    factor_of = 1.0
    for dim, shards_of in pieces:
        heights = jax.random.uniform(jax.random.fold_in(jax.random.fold_in(rng, 6), dim), (shards_of,), jnp.float32, smallest / len(pieces), largest / len(pieces))
        factor_of = factor_of * jnp.repeat(jnp.exp(heights), extent[dim] // shards_of).reshape((-1,) + (1,) * (len(extent) - 1 - dim))
    return factor_of


def centred(own_key, extent, scale, bound, shards=(), kind=jnp.bfloat16):
    entries = scale * jax.random.normal(own_key, extent, jnp.float32)
    if shards:
        entries = entries * level_of(own_key, extent, shards, -0.22, 0.18)
    return jnp.clip(entries, -bound, bound).astype(kind)


def setup_inputs(seed: int = 0) -> dict:
    keys = jax.random.split(jax.random.key(seed), 8)
    tokens = draw_tokens(jax.random.fold_in(keys[7], 71), 0)
    norm_gain = jnp.clip(1.0 + 0.18 * jax.random.normal(keys[1], (D,), jnp.float32), 0.1, 1.9)
    norm_bias = centred(keys[2], (D,), 0.5, 3.0, (), jnp.float32)
    routes = draw_routes(jax.random.fold_in(keys[7], 71), 0)
    gate_codes = with_ends(jax.random.randint(keys[4], (TOKENS, TOP), 1, 1024), jax.random.fold_in(keys[4], 1), 1, 1023).astype(jnp.int32)
    w_in = centred(keys[5], (EXPERTS, D, 2 * FF), D ** -0.5, 0.125, ((0, 8),))
    w_out = centred(keys[6], (EXPERTS, FF, D), FF ** -0.5, 0.21875, ((0, 8),))
    return {"tokens": tokens, "norm_gain": norm_gain, "norm_bias": norm_bias, "routes": routes, "gate_codes": gate_codes, "w_in": w_in, "w_out": w_out}


def layer_norm(tokens, norm_gain, norm_bias):
    values = tokens.astype(jnp.float32)
    average = lax.optimization_barrier(jnp.mean(values, axis=1, keepdims=True))
    centered = values - average
    variance = lax.optimization_barrier(jnp.mean(centered * centered, axis=1, keepdims=True))
    return (centered * lax.rsqrt(variance + 1e-05) * norm_gain + norm_bias).astype(jnp.bfloat16)

def expert_rows(inputs, weight_in, weight_out):
    inner_width = weight_out.shape[0]
    projected = jnp.dot(inputs, weight_in, preferred_element_type=jnp.float32)
    hidden = (jax.nn.silu(projected[:, :inner_width]) * projected[:, inner_width:]).astype(jnp.bfloat16)
    return jnp.dot(hidden, weight_out, preferred_element_type=jnp.float32).astype(jnp.bfloat16)

def rank_in_block(block_ids):
    one_hot = (block_ids[:, None] == jnp.arange(EXPERTS, dtype=jnp.int32)[None, :]).astype(jnp.int32)
    earlier = (jnp.cumsum(one_hot, axis=0) - one_hot).astype(jnp.int32)
    return lax.optimization_barrier(jnp.sum(earlier * one_hot, axis=1)).astype(jnp.int32)

def find_hot(block_ids):
    one_hot = (block_ids[:, None] == jnp.arange(EXPERTS, dtype=jnp.int32)[None, :]).astype(jnp.int32)
    counts = lax.optimization_barrier(jnp.sum(one_hot, axis=0)).astype(jnp.int32)
    return jnp.argmax(counts).astype(jnp.int32)

def reference(tokens, norm_gain, norm_bias, routes, gate_codes, w_in, w_out):
    normed = layer_norm(tokens, norm_gain, norm_bias)
    total, features = normed.shape
    blocks = total // TOK_DEV
    slot_total = EXPERTS * CAP
    block_ids = routes.reshape(blocks, TOK_DEV * TOP)
    hot_expert = find_hot(block_ids[0])
    gate_vals = gate_codes.astype(jnp.float32) * (1.0 / 1024.0)
    slot_rank = lax.map(rank_in_block, block_ids)
    kept_mask = (block_ids != hot_expert) & (slot_rank < CAP)
    slot_index = jnp.where(kept_mask, block_ids * CAP + slot_rank, slot_total).astype(jnp.int32)
    local_token = jnp.arange(TOK_DEV * TOP, dtype=jnp.int32) // TOP
    block_start = jnp.arange(blocks, dtype=jnp.int32) * TOK_DEV
    token_index = (local_token[None, :] + block_start[:, None]).astype(jnp.int32)

    def place_block(indices, owner_tokens, weights):
        token_table = jnp.full((slot_total,), total, jnp.int32).at[indices].set(owner_tokens, mode='drop')
        gate_table = jnp.zeros((slot_total,), jnp.float32).at[indices].set(weights, mode='drop')
        return (token_table, gate_table)
    slot_token, slot_gate = jax.vmap(place_block)(slot_index, token_index, gate_vals.reshape(blocks, TOK_DEV * TOP))
    slot_token = slot_token.reshape(blocks, EXPERTS, CAP).transpose(1, 0, 2).reshape(EXPERTS, blocks * CAP)
    slot_gate = slot_gate.reshape(blocks, EXPERTS, CAP).transpose(1, 0, 2).reshape(EXPERTS, blocks * CAP)
    padded_rows = jnp.concatenate([normed, jnp.zeros((1, features), normed.dtype)], axis=0)

    def add_expert(running, item):
        token_list, gate_list, weight_in, weight_out = item
        results = expert_rows(padded_rows[token_list], weight_in, weight_out)
        return (running.at[token_list].add(gate_list[:, None] * results.astype(jnp.float32), mode='drop'), None)
    routed = lax.scan(add_expert, jnp.zeros((total, features), jnp.float32), (slot_token, slot_gate, w_in, w_out))[0]
    hot_weight = lax.optimization_barrier(jnp.sum(jnp.where(routes == hot_expert, gate_vals, 0.0), axis=1))
    hot_in = w_in[hot_expert]
    hot_down = w_out[hot_expert]

    def hot_block(block_rows):
        return expert_rows(block_rows, hot_in, hot_down)
    hot_rows = lax.map(hot_block, normed.reshape(blocks, TOK_DEV, features)).reshape(total, features)
    return (routed + hot_weight[:, None] * hot_rows.astype(jnp.float32)).astype(jnp.bfloat16)
```

```python
import jax
import jax.numpy as jnp
from jax import lax
from jax.sharding import PartitionSpec as P


def layer_norm(tokens, norm_gain, norm_bias):
    values = tokens.astype(jnp.float32)
    average = jnp.mean(values, axis=1, keepdims=True)
    centered = values - average
    variance = jnp.mean(centered * centered, axis=1, keepdims=True)
    return (centered * lax.rsqrt(variance + 1e-05) * norm_gain + norm_bias).astype(jnp.bfloat16)


def row_codes(routes, gate_codes, owners, capacity):
    rows = routes.shape[0]
    match = routes[:, :, None] == jnp.arange(owners, dtype=jnp.int32)[None, None, :]
    codes = jnp.sum(jnp.where(match, gate_codes[:, :, None], 0), axis=1).astype(jnp.float32)
    named = jnp.any(match, axis=1)
    before = lax.broadcasted_iota(jnp.int32, (rows, rows), 1) < lax.broadcasted_iota(
        jnp.int32, (rows, rows), 0
    )
    named_b = named.astype(jnp.bfloat16)
    rank = jnp.dot(before.astype(jnp.bfloat16), named_b, preferred_element_type=jnp.float32)
    hot = jnp.argmax(jnp.sum(named.astype(jnp.float32), axis=0))
    kept = (rank < capacity) | (jnp.arange(owners)[None, :] == hot)
    return jnp.where(kept, codes, 0.0)


def local(tokens, norm_gain, norm_bias, routes, gate_codes, w_in, w_out):
    owners = lax.axis_size("exp")
    rows = tokens.shape[0]
    capacity = min(rows, rows * routes.shape[1] * 9 // (8 * owners))
    normed = layer_norm(tokens, norm_gain, norm_bias)
    codes = row_codes(routes, gate_codes, owners, capacity)
    all_rows = lax.all_gather(normed, "exp", axis=0, tiled=True)
    all_codes = lax.all_gather(codes, "exp", axis=0, tiled=True)
    me = lax.axis_index("exp")
    weight = lax.dynamic_slice_in_dim(all_codes, me, 1, 1) * (1.0 / 1024.0)
    inner = w_out.shape[1]
    projected = jnp.dot(all_rows, w_in[0], preferred_element_type=jnp.float32)
    hidden = (jax.nn.silu(projected[:, :inner]) * projected[:, inner:]).astype(jnp.bfloat16)
    results = jnp.dot(hidden, w_out[0], preferred_element_type=jnp.float32)
    part = (results * weight).astype(jnp.bfloat16)
    return lax.psum_scatter(part, "exp", scatter_dimension=0, tiled=True)


def solution(mesh):
    return jax.shard_map(
        local,
        mesh=mesh,
        in_specs=(
            P(("seq", "exp"), None),
            P(),
            P(),
            P(("seq", "exp"), None),
            P(("seq", "exp"), None),
            P("exp", None, None),
            P("exp", None, None),
        ),
        out_specs=P(("seq", "exp"), None),
        check_vma=False,
    )
```

```python
import jax
import jax.numpy as jnp
from jax import lax
from jax.experimental import pallas as pl
from jax.experimental.pallas import tpu as pltpu
from jax.sharding import PartitionSpec as P


def layer_norm(tokens, norm_gain, norm_bias):
    values = tokens.astype(jnp.float32)
    average = jnp.mean(values, axis=1, keepdims=True)
    centered = values - average
    variance = jnp.mean(centered * centered, axis=1, keepdims=True)
    return (centered * lax.rsqrt(variance + 1e-05) * norm_gain + norm_bias).astype(jnp.bfloat16)


def row_codes(routes, gate_codes, owners, capacity):
    rows = routes.shape[0]
    match = routes[:, :, None] == jnp.arange(owners, dtype=jnp.int32)[None, None, :]
    codes = jnp.sum(jnp.where(match, gate_codes[:, :, None], 0), axis=1).astype(jnp.float32)
    named = jnp.any(match, axis=1)
    before = lax.broadcasted_iota(jnp.int32, (rows, rows), 1) < lax.broadcasted_iota(
        jnp.int32, (rows, rows), 0
    )
    named_b = named.astype(jnp.bfloat16)
    rank = jnp.dot(before.astype(jnp.bfloat16), named_b, preferred_element_type=jnp.float32)
    hot = jnp.argmax(jnp.sum(named.astype(jnp.float32), axis=0))
    kept = (rank < capacity) | (jnp.arange(owners)[None, :] == hot)
    return jnp.where(kept, codes, 0.0)


LANES = 128
STEP = 16


def fused(
    owners, top, capacity, tokens, gain, bias, routes, gates, w_in_hbm, w_out_hbm, out,
    rows_all, codes, part, sib, from_x, from_y, diag_in, proj, hid, weight, w_in, w_out,
    load_sem, send_sem, recv_sem,
):
    n = tokens.shape[0]
    half = n // 2
    width = tokens.shape[1]
    inner = w_out.shape[0]
    me = lax.axis_index("exp")
    core, across, along = me % 2, me // 2 % 2, me // 4

    def peer(rel):
        c = 1 - core if rel % 2 else core
        x = 1 - across if rel // 2 % 2 else across
        y = 1 - along if rel // 4 else along
        return {"exp": y * 4 + x * 2 + c}

    sibling, x_near, y_near = 1, 2, 4

    def move(index, src, dst, rel):
        return pltpu.make_async_remote_copy(
            src_ref=src,
            dst_ref=dst,
            send_sem=send_sem.at[index],
            recv_sem=recv_sem.at[index],
            device_id=peer(rel),
            device_id_type=pl.DeviceIdType.MESH,
        )

    first, second = pl.ds(0, n), pl.ds(n, n)
    upper, lower = pl.ds(0, half), pl.ds(half, half)
    load_in = pltpu.make_async_copy(w_in_hbm.at[0], w_in, load_sem.at[0])
    load_out = pltpu.make_async_copy(w_out_hbm.at[0], w_out, load_sem.at[1])
    load_in.start()
    load_out.start()
    barrier = pltpu.get_barrier_semaphore()
    for rel in range(1, 8):
        pl.semaphore_signal(
            barrier, inc=1, device_id=peer(rel), device_id_type=pl.DeviceIdType.MESH
        )

    @pl.loop(0, n // STEP)
    def _(i):
        at = pl.ds(pl.multiple_of(i * STEP, STEP), STEP)
        values = tokens[at, :].astype(jnp.float32)
        average = jnp.mean(values, axis=1, keepdims=True)
        centered = values - average
        variance = jnp.mean(centered * centered, axis=1, keepdims=True)
        scaled = centered * lax.rsqrt(variance + 1e-05) * gain[...] + bias[...]
        rows_all[0, at, :] = scaled.astype(jnp.bfloat16)

    pl.semaphore_wait(barrier, 7)
    to_x = move(0, rows_all.at[0, first], rows_all.at[1, first], x_near)
    to_y = move(1, rows_all.at[0, first], rows_all.at[2, first], y_near)
    to_sib = move(2, rows_all.at[0, first], rows_all.at[0, second], sibling)
    to_sib.start()
    to_x.start()
    to_y.start()

    lane = lax.broadcasted_iota(jnp.int32, (n, LANES), 1)
    code = jnp.zeros((n, LANES), jnp.int32)
    named = jnp.zeros((n, LANES), jnp.float32)
    for j in range(top):
        match = routes[:, j : j + 1] == lane
        code = code + jnp.where(match, gates[:, j : j + 1], 0)
        named = named + jnp.where(match, 1.0, 0.0)
    before = jnp.where(
        lax.broadcasted_iota(jnp.int32, (n, n), 1) < lax.broadcasted_iota(jnp.int32, (n, n), 0),
        1.0,
        0.0,
    ).astype(jnp.bfloat16)
    rank = jnp.dot(before, named.astype(jnp.bfloat16), preferred_element_type=jnp.float32)
    counts = jnp.sum(named, axis=0, keepdims=True)
    most = jnp.max(counts, axis=1, keepdims=True)
    lane_row = lane[0:1, :].astype(jnp.float32)
    hot = jnp.min(jnp.where(counts == most, lane_row, 1e9), axis=1, keepdims=True)
    keep = jnp.where(lane_row == hot, 1e9, float(capacity))
    code = jnp.where(rank < keep, code, 0)
    low = code % 4
    high = code - low
    row16 = lax.broadcasted_iota(jnp.int32, (2 * owners, LANES), 0)
    lane16 = lax.broadcasted_iota(jnp.int32, (2 * owners, LANES), 1)

    def turned(pick, value):
        return lax.dot_general(
            jnp.where(pick, 1.0, 0.0).astype(jnp.bfloat16),
            value.astype(jnp.float32).astype(jnp.bfloat16),
            (((1,), (1,)), ((), ())),
            preferred_element_type=jnp.float32,
        )

    both = turned(row16 == lane16, high) + turned(row16 == lane16 + owners, low)
    codes[0] = jnp.zeros(codes.shape[1:], jnp.bfloat16)
    codes[0, :, 0:n] = both.astype(jnp.bfloat16)
    code_moves = [None] + [move(7 + rel, codes.at[0], codes.at[rel], rel) for rel in range(1, 8)]
    for rel in range(1, 8):
        code_moves[rel].start()

    choose = jnp.where((row16 == me) | (row16 == me + owners), 1.0, 0.0).astype(jnp.bfloat16)

    def expert(k):
        for c in range(2):
            column = lax.dot_general(
                codes[2 * k + c],
                choose,
                (((0,), (0,)), ((), ())),
                preferred_element_type=jnp.float32,
            )
            weight[c * n : (c + 1) * n, :] = column[0:n, :] * (1.0 / 1024.0)

        full = 2 * inner // 256

        @pl.loop(0, full)
        def _(i):
            at = pl.ds(pl.multiple_of(i * 256, 256), 256)
            proj[:, at] = jnp.dot(
                rows_all[k], w_in[:, at], preferred_element_type=jnp.float32
            )

        if full * 256 < 2 * inner:
            rest = pl.ds(full * 256, 2 * inner - full * 256)
            proj[:, rest] = jnp.dot(
                rows_all[k], w_in[:, rest], preferred_element_type=jnp.float32
            )

        wide = -(-inner // LANES) * LANES

        @pl.loop(0, 2 * n // STEP)
        def _(i):
            at = pl.ds(pl.multiple_of(i * STEP, STEP), STEP)
            a = proj[at, :]
            b = pltpu.roll(a, inner, 1)[:, :wide]
            a = a[:, :wide]
            hid[at, :] = (a / (1.0 + jnp.exp(-a)) * b)[:, :inner].astype(jnp.bfloat16)

        @pl.loop(0, width // 256)
        def _(i):
            at = pl.ds(pl.multiple_of(i * 256, 256), 256)
            y = jnp.dot(hid[...], w_out[:, at], preferred_element_type=jnp.float32)
            scale = weight[...]
            part[k, :, at] = (y * jnp.concatenate([scale, scale], axis=1)).astype(jnp.bfloat16)

    def add(dst, terms, count):
        @pl.loop(0, count // STEP)
        def _(i):
            at = pl.ds(pl.multiple_of(i * STEP, STEP), STEP)
            total = terms[0][at, :].astype(jnp.float32)
            for term in terms[1:]:
                total = total + term[at, :].astype(jnp.float32)
            dst[at, :] = total.astype(jnp.bfloat16)

    part_moves = [move(15 + k, part.at[k, second], sib.at[k], sibling) for k in range(4)]
    x_sib = move(3, rows_all.at[1, first], rows_all.at[1, second], sibling)
    y_sib = move(4, rows_all.at[2, first], rows_all.at[2, second], sibling)
    x_on = move(5, rows_all.at[1, upper], rows_all.at[3, upper], y_near)
    y_on = move(6, rows_all.at[2, lower], rows_all.at[3, lower], x_near)
    d_sib = move(7, rows_all.at[3, first], rows_all.at[3, second], sibling)
    x_up = move(19, part.at[1, upper], from_x.at[upper], x_near)
    y_low = move(20, part.at[2, lower], from_y.at[lower], y_near)
    d_up = move(21, part.at[3, upper], diag_in.at[upper], x_near)
    d_low = move(22, part.at[3, lower], diag_in.at[lower], y_near)
    x_low = move(23, part.at[1, lower], from_x.at[lower], x_near)
    y_up = move(24, part.at[2, upper], from_y.at[upper], y_near)

    def chip_sum(k):
        part_moves[k].wait_recv()
        mine = part.at[k, first]
        add(mine, [mine, sib.at[k]], n)

    load_in.wait()
    load_out.wait()
    to_sib.wait_recv()
    code_moves[1].wait_recv()
    expert(0)
    part_moves[0].start()
    to_x.wait_recv()
    x_sib.start()
    x_on.start()
    to_y.wait_recv()
    y_sib.start()
    y_on.start()
    code_moves[2].wait_recv()
    code_moves[3].wait_recv()
    x_sib.wait_recv()
    expert(1)
    part_moves[1].start()
    y_sib.wait_recv()
    code_moves[4].wait_recv()
    code_moves[5].wait_recv()
    chip_sum(1)
    x_up.start()
    expert(2)
    part_moves[2].start()
    x_on.wait_recv()
    y_on.wait_recv()
    d_sib.start()
    code_moves[6].wait_recv()
    code_moves[7].wait_recv()
    chip_sum(2)
    y_low.start()
    d_sib.wait_recv()
    expert(3)
    part_moves[3].start()
    chip_sum(3)
    d_up.start()
    d_low.start()
    chip_sum(0)
    d_up.wait_recv()
    theirs = part.at[2, upper]
    add(theirs, [theirs, diag_in.at[upper]], half)
    y_up.start()
    d_low.wait_recv()
    theirs = part.at[1, lower]
    add(theirs, [theirs, diag_in.at[lower]], half)
    x_low.start()
    x_up.wait_recv()
    y_low.wait_recv()
    y_up.wait_recv()
    x_low.wait_recv()
    add(out, [part.at[0, first], from_x, from_y], n)
    for sent in (
        [to_x, to_y, to_sib, x_sib, y_sib, x_on, y_on, d_sib]
        + code_moves[1:]
        + part_moves
        + [x_up, y_low, d_up, d_low, x_low, y_up]
    ):
        sent.wait_send()


def fused_call(tokens, norm_gain, norm_bias, routes, gate_codes, w_in, w_out, capacity):
    owners = lax.axis_size("exp")
    n, width = tokens.shape
    inner = w_out.shape[1]
    top = routes.shape[1]
    vmem = pl.BlockSpec(memory_space=pltpu.VMEM)
    anywhere = pl.BlockSpec(memory_space=pl.ANY)
    bf16, f32 = jnp.bfloat16, jnp.float32

    def body(*refs):
        fused(owners, top, capacity, *refs)

    flops = 2 * owners * n * width * inner * 3
    return pl.pallas_call(
        body,
        out_shape=jax.ShapeDtypeStruct((n, width), bf16),
        in_specs=[vmem] * 5 + [anywhere] * 2,
        out_specs=vmem,
        scratch_shapes=[
            pltpu.VMEM((4, 2 * n, width), bf16),
            pltpu.VMEM((8, 2 * owners, -(-n // LANES) * LANES), bf16),
            pltpu.VMEM((4, 2 * n, width), bf16),
            pltpu.VMEM((4, n, width), bf16),
            pltpu.VMEM((n, width), bf16),
            pltpu.VMEM((n, width), bf16),
            pltpu.VMEM((n, width), bf16),
            pltpu.VMEM((2 * n, 2 * inner), f32),
            pltpu.VMEM((2 * n, inner), bf16),
            pltpu.VMEM((2 * n, LANES), f32),
            pltpu.VMEM((width, 2 * inner), bf16),
            pltpu.VMEM((inner, width), bf16),
            pltpu.SemaphoreType.DMA((2,)),
            pltpu.SemaphoreType.DMA((25,)),
            pltpu.SemaphoreType.DMA((25,)),
        ],
        compiler_params=pltpu.CompilerParams(
            collective_id=0, has_side_effects=True, vmem_limit_bytes=56 * 2**20
        ),
        cost_estimate=pl.CostEstimate(
            flops=flops, bytes_accessed=6 * width * inner, transcendentals=owners * n * inner
        ),
    )(tokens, norm_gain[None, :], norm_bias[None, :], routes, gate_codes, w_in, w_out)


def local(tokens, norm_gain, norm_bias, routes, gate_codes, w_in, w_out):
    owners = lax.axis_size("exp")
    rows = tokens.shape[0]
    capacity = min(rows, rows * routes.shape[1] * 9 // (8 * owners))
    if owners == 8:
        return fused_call(
            tokens, norm_gain, norm_bias, routes, gate_codes, w_in, w_out, capacity
        )
    normed = layer_norm(tokens, norm_gain, norm_bias)
    codes = row_codes(routes, gate_codes, owners, capacity)
    all_rows = lax.all_gather(normed, "exp", axis=0, tiled=True)
    all_codes = lax.all_gather(codes, "exp", axis=0, tiled=True)
    me = lax.axis_index("exp")
    weight = lax.dynamic_slice_in_dim(all_codes, me, 1, 1) * (1.0 / 1024.0)
    inner = w_out.shape[1]
    projected = jnp.dot(all_rows, w_in[0], preferred_element_type=jnp.float32)
    hidden = (jax.nn.silu(projected[:, :inner]) * projected[:, inner:]).astype(jnp.bfloat16)
    results = jnp.dot(hidden, w_out[0], preferred_element_type=jnp.float32)
    part = (results * weight).astype(jnp.bfloat16)
    return lax.psum_scatter(part, "exp", scatter_dimension=0, tiled=True)


def solution(mesh):
    return jax.shard_map(
        local,
        mesh=mesh,
        in_specs=(
            P(("seq", "exp"), None),
            P(),
            P(),
            P(("seq", "exp"), None),
            P(("seq", "exp"), None),
            P("exp", None, None),
            P("exp", None, None),
        ),
        out_specs=P(("seq", "exp"), None),
        check_vma=False,
    )
```

```python
import jax
import jax.numpy as jnp
from jax import lax
from jax.experimental import pallas as pl
from jax.experimental.pallas import tpu as pltpu
from jax.sharding import PartitionSpec as P


def layer_norm(tokens, norm_gain, norm_bias):
    values = tokens.astype(jnp.float32)
    average = jnp.mean(values, axis=1, keepdims=True)
    centered = values - average
    variance = jnp.mean(centered * centered, axis=1, keepdims=True)
    return (centered * lax.rsqrt(variance + 1e-05) * norm_gain + norm_bias).astype(jnp.bfloat16)


def row_codes(routes, gate_codes, owners, capacity):
    rows = routes.shape[0]
    match = routes[:, :, None] == jnp.arange(owners, dtype=jnp.int32)[None, None, :]
    codes = jnp.sum(jnp.where(match, gate_codes[:, :, None], 0), axis=1).astype(jnp.float32)
    named = jnp.any(match, axis=1)
    before = lax.broadcasted_iota(jnp.int32, (rows, rows), 1) < lax.broadcasted_iota(
        jnp.int32, (rows, rows), 0
    )
    named_b = named.astype(jnp.bfloat16)
    rank = jnp.dot(before.astype(jnp.bfloat16), named_b, preferred_element_type=jnp.float32)
    hot = jnp.argmax(jnp.sum(named.astype(jnp.float32), axis=0))
    kept = (rank < capacity) | (jnp.arange(owners)[None, :] == hot)
    return jnp.where(kept, codes, 0.0)


LANES = 128
STEP = 16


def fused(
    owners, top, capacity, tokens, gain, bias, routes, gates, w_in_hbm, w_out_hbm, out,
    rows_all, codes, part, sib, from_x, from_y, diag_in, hid, weight, w_in, w_up, w_out,
    load_sem, send_sem, recv_sem,
):
    n = tokens.shape[0]
    half = n // 2
    width = tokens.shape[1]
    inner = w_out.shape[0]
    me = lax.axis_index("exp")
    core, across, along = me % 2, me // 2 % 2, me // 4

    def peer(rel):
        c = 1 - core if rel % 2 else core
        x = 1 - across if rel // 2 % 2 else across
        y = 1 - along if rel // 4 else along
        return {"exp": y * 4 + x * 2 + c}

    sibling, x_near, y_near = 1, 2, 4

    def move(index, src, dst, rel):
        return pltpu.make_async_remote_copy(
            src_ref=src,
            dst_ref=dst,
            send_sem=send_sem.at[index],
            recv_sem=recv_sem.at[index],
            device_id=peer(rel),
            device_id_type=pl.DeviceIdType.MESH,
        )

    first, second = pl.ds(0, n), pl.ds(n, n)
    upper, lower = pl.ds(0, half), pl.ds(half, half)
    load_in = pltpu.make_async_copy(w_in_hbm.at[0], w_in, load_sem.at[0])
    load_out = pltpu.make_async_copy(w_out_hbm.at[0], w_out, load_sem.at[1])
    load_in.start()
    load_out.start()
    barrier = pltpu.get_barrier_semaphore()
    for rel in range(1, 8):
        pl.semaphore_signal(
            barrier, inc=1, device_id=peer(rel), device_id_type=pl.DeviceIdType.MESH
        )

    @pl.loop(0, n // STEP)
    def _(i):
        at = pl.ds(pl.multiple_of(i * STEP, STEP), STEP)
        values = tokens[at, :].astype(jnp.float32)
        average = jnp.mean(values, axis=1, keepdims=True)
        centered = values - average
        variance = jnp.mean(centered * centered, axis=1, keepdims=True)
        scaled = centered * lax.rsqrt(variance + 1e-05) * gain[...] + bias[...]
        rows_all[0, at, :] = scaled.astype(jnp.bfloat16)

    pl.semaphore_wait(barrier, 7)
    a_x = move(0, rows_all.at[0, upper], rows_all.at[1, upper], x_near)
    b_y = move(1, rows_all.at[0, lower], rows_all.at[1, lower], y_near)
    to_sib = move(2, rows_all.at[0, first], rows_all.at[0, second], sibling)
    a_x.start()
    b_y.start()
    to_sib.start()

    expert_row = lax.broadcasted_iota(jnp.int32, (owners, n), 0)
    code = jnp.zeros((owners, n), jnp.int32)
    named = jnp.zeros((owners, n), jnp.float32)
    for j in range(top):
        match = routes[j : j + 1, :] == expert_row
        code = code + jnp.where(match, gates[j : j + 1, :], 0)
        named = named + jnp.where(match, 1.0, 0.0)
    before = jnp.where(
        lax.broadcasted_iota(jnp.int32, (n, n), 0) < lax.broadcasted_iota(jnp.int32, (n, n), 1),
        1.0,
        0.0,
    ).astype(jnp.bfloat16)
    rank = jnp.dot(named.astype(jnp.bfloat16), before, preferred_element_type=jnp.float32)
    counts = jnp.sum(named, axis=1, keepdims=True)
    most = jnp.max(counts, axis=0, keepdims=True)
    index = expert_row.astype(jnp.float32)
    hot = jnp.min(jnp.where(counts == most, index, 1e9), axis=0, keepdims=True)
    code = jnp.where((rank < capacity) | (index == hot), code, 0)
    low = code % 4
    both = jnp.concatenate([code - low, low], axis=0).astype(jnp.float32)
    codes[0] = jnp.zeros(codes.shape[1:], jnp.bfloat16)
    codes[0, :, 0:n] = both.astype(jnp.bfloat16)
    code_moves = [None] + [move(7 + rel, codes.at[0], codes.at[rel], rel) for rel in range(1, 8)]
    for rel in range(1, 8):
        code_moves[rel].start()

    row16 = lax.broadcasted_iota(jnp.int32, (2 * owners, LANES), 0)
    choose = jnp.where((row16 == me) | (row16 == me + owners), 1.0, 0.0).astype(jnp.bfloat16)

    up_width = w_up.shape[1]

    def expert(k):
        if k == 0:
            pieces = ((0, 0, 0, n), (n, 1, 0, n))
        elif k == 2:
            pieces = ((0, 6, 0, n), (n, 7, 0, n))
        else:
            x_from, y_from = (0, half) if k == 1 else (half, 0)
            pieces = (
                (0, 2, x_from, half), (half, 4, y_from, half),
                (n, 3, x_from, half), (n + half, 5, y_from, half),
            )
        for at, slot, start, count in pieces:
            column = lax.dot_general(
                codes[slot],
                choose,
                (((0,), (0,)), ((), ())),
                preferred_element_type=jnp.float32,
            )
            weight[at : at + count, :] = column[start : start + count, :] * (1.0 / 1024.0)

        @pl.loop(0, up_width // 256)
        def _(i):
            at = pl.ds(pl.multiple_of(i * 256, 256), 256)
            a = jnp.dot(rows_all[k], w_in[:, at], preferred_element_type=jnp.float32)
            b = jnp.dot(rows_all[k], w_up[:, at], preferred_element_type=jnp.float32)
            hid[:, at] = (a / (1.0 + jnp.exp(-a)) * b).astype(jnp.bfloat16)

        @pl.loop(0, width // 256)
        def _(i):
            at = pl.ds(pl.multiple_of(i * 256, 256), 256)
            y = jnp.dot(hid[:, :inner], w_out[:, at], preferred_element_type=jnp.float32)
            scale = weight[...]
            part[k, :, at] = (y * jnp.concatenate([scale, scale], axis=1)).astype(jnp.bfloat16)

    def add(dst, terms, count):
        @pl.loop(0, count // STEP)
        def _(i):
            at = pl.ds(pl.multiple_of(i * STEP, STEP), STEP)
            total = terms[0][at, :].astype(jnp.float32)
            for term in terms[1:]:
                total = total + term[at, :].astype(jnp.float32)
            dst[at, :] = total.astype(jnp.bfloat16)

    part_moves = [move(3 + k, part.at[k, second], sib.at[k], sibling) for k in range(4)]
    row_sib = [None] + [
        move(14 + k, rows_all.at[k, first], rows_all.at[k, second], sibling) for k in range(1, 4)
    ]
    x_on = move(18, rows_all.at[1, upper], rows_all.at[2, upper], y_near)
    y_on = move(19, rows_all.at[1, lower], rows_all.at[2, lower], x_near)
    b_x = move(20, rows_all.at[0, lower], rows_all.at[3, upper], x_near)
    a_y = move(21, rows_all.at[0, upper], rows_all.at[3, lower], y_near)
    sum_a_x = move(22, part.at[1, upper], from_x.at[upper], x_near)
    sum_b_y = move(23, part.at[1, lower], from_y.at[lower], y_near)
    sum_d_x = move(24, part.at[2, upper], diag_in.at[upper], x_near)
    sum_d_y = move(25, part.at[2, lower], diag_in.at[lower], y_near)
    sum_b_x = move(26, part.at[3, upper], from_x.at[lower], x_near)
    sum_a_y = move(27, part.at[3, lower], from_y.at[upper], y_near)

    load_in.wait()

    @pl.loop(0, width // STEP)
    def _(i):
        at = pl.ds(pl.multiple_of(i * STEP, STEP), STEP)
        turned_in = pltpu.roll(w_in[at, :].astype(jnp.float32), inner, 1)
        w_up[at, :] = turned_in[:, :up_width].astype(jnp.bfloat16)

    load_out.wait()
    to_sib.wait_recv()
    code_moves[1].wait_recv()
    expert(0)
    part_moves[0].start()
    a_x.wait_recv()
    x_on.start()
    b_y.wait_recv()
    y_on.start()
    row_sib[1].start()
    b_x.start()
    a_y.start()
    for rel in range(2, 8):
        code_moves[rel].wait_recv()
    row_sib[1].wait_recv()
    expert(1)
    part_moves[1].start()
    part_moves[1].wait_recv()
    mine = part.at[1, first]
    add(mine, [mine, sib.at[1]], n)
    sum_a_x.start()
    sum_b_y.start()
    x_on.wait_recv()
    y_on.wait_recv()
    row_sib[2].start()
    row_sib[2].wait_recv()
    expert(2)
    part_moves[2].start()
    part_moves[2].wait_recv()
    mine = part.at[2, first]
    add(mine, [mine, sib.at[2]], n)
    sum_d_x.start()
    sum_d_y.start()
    b_x.wait_recv()
    a_y.wait_recv()
    row_sib[3].start()
    row_sib[3].wait_recv()
    expert(3)
    part_moves[3].start()
    part_moves[3].wait_recv()
    sum_d_x.wait_recv()
    mine = part.at[3, lower]
    add(mine, [mine, sib.at[3, lower], diag_in.at[upper]], half)
    sum_a_y.start()
    sum_d_y.wait_recv()
    mine = part.at[3, upper]
    add(mine, [mine, sib.at[3, upper], diag_in.at[lower]], half)
    sum_b_x.start()
    part_moves[0].wait_recv()
    sum_a_x.wait_recv()
    sum_b_y.wait_recv()
    sum_a_y.wait_recv()
    sum_b_x.wait_recv()
    add(out, [part.at[0, first], sib.at[0], from_x, from_y], n)
    for sent in (
        [a_x, b_y, to_sib, x_on, y_on, b_x, a_y]
        + row_sib[1:]
        + code_moves[1:]
        + part_moves
        + [sum_a_x, sum_b_y, sum_d_x, sum_d_y, sum_b_x, sum_a_y]
    ):
        sent.wait_send()


def fused_call(tokens, norm_gain, norm_bias, routes, gate_codes, w_in, w_out, capacity):
    owners = lax.axis_size("exp")
    n, width = tokens.shape
    inner = w_out.shape[1]
    top = routes.shape[1]
    wide = -(-inner // 256) * 256
    vmem = pl.BlockSpec(memory_space=pltpu.VMEM)
    anywhere = pl.BlockSpec(memory_space=pl.ANY)
    bf16, f32 = jnp.bfloat16, jnp.float32

    def body(*refs):
        fused(owners, top, capacity, *refs)

    flops = 2 * owners * n * width * inner * 3
    return pl.pallas_call(
        body,
        out_shape=jax.ShapeDtypeStruct((n, width), bf16),
        in_specs=[vmem] * 5 + [anywhere] * 2,
        out_specs=vmem,
        scratch_shapes=[
            pltpu.VMEM((4, 2 * n, width), bf16),
            pltpu.VMEM((8, 2 * owners, -(-n // LANES) * LANES), bf16),
            pltpu.VMEM((4, 2 * n, width), bf16),
            pltpu.VMEM((4, n, width), bf16),
            pltpu.VMEM((n, width), bf16),
            pltpu.VMEM((n, width), bf16),
            pltpu.VMEM((n, width), bf16),
            pltpu.VMEM((2 * n, wide), bf16),
            pltpu.VMEM((2 * n, LANES), f32),
            pltpu.VMEM((width, 2 * inner), bf16),
            pltpu.VMEM((width, wide), bf16),
            pltpu.VMEM((inner, width), bf16),
            pltpu.SemaphoreType.DMA((2,)),
            pltpu.SemaphoreType.DMA((28,)),
            pltpu.SemaphoreType.DMA((28,)),
        ],
        compiler_params=pltpu.CompilerParams(
            collective_id=0, has_side_effects=True, vmem_limit_bytes=56 * 2**20
        ),
        cost_estimate=pl.CostEstimate(
            flops=flops, bytes_accessed=6 * width * inner, transcendentals=owners * n * inner
        ),
    )(tokens, norm_gain[None, :], norm_bias[None, :], routes.T, gate_codes.T, w_in, w_out)


def local(tokens, norm_gain, norm_bias, routes, gate_codes, w_in, w_out):
    owners = lax.axis_size("exp")
    rows = tokens.shape[0]
    capacity = min(rows, rows * routes.shape[1] * 9 // (8 * owners))
    if owners == 8:
        return fused_call(
            tokens, norm_gain, norm_bias, routes, gate_codes, w_in, w_out, capacity
        )
    normed = layer_norm(tokens, norm_gain, norm_bias)
    codes = row_codes(routes, gate_codes, owners, capacity)
    all_rows = lax.all_gather(normed, "exp", axis=0, tiled=True)
    all_codes = lax.all_gather(codes, "exp", axis=0, tiled=True)
    me = lax.axis_index("exp")
    weight = lax.dynamic_slice_in_dim(all_codes, me, 1, 1) * (1.0 / 1024.0)
    inner = w_out.shape[1]
    projected = jnp.dot(all_rows, w_in[0], preferred_element_type=jnp.float32)
    hidden = (jax.nn.silu(projected[:, :inner]) * projected[:, inner:]).astype(jnp.bfloat16)
    results = jnp.dot(hidden, w_out[0], preferred_element_type=jnp.float32)
    part = (results * weight).astype(jnp.bfloat16)
    return lax.psum_scatter(part, "exp", scatter_dimension=0, tiled=True)


def solution(mesh):
    return jax.shard_map(
        local,
        mesh=mesh,
        in_specs=(
            P(("seq", "exp"), None),
            P(),
            P(),
            P(("seq", "exp"), None),
            P(("seq", "exp"), None),
            P("exp", None, None),
            P("exp", None, None),
        ),
        out_specs=P(("seq", "exp"), None),
        check_vma=False,
    )
```

```python
import jax
import jax.numpy as jnp
from jax import lax
from jax.experimental import pallas as pl
from jax.experimental.pallas import tpu as pltpu
from jax.sharding import PartitionSpec as P


def layer_norm(tokens, norm_gain, norm_bias):
    values = tokens.astype(jnp.float32)
    average = jnp.mean(values, axis=1, keepdims=True)
    centered = values - average
    variance = jnp.mean(centered * centered, axis=1, keepdims=True)
    return (centered * lax.rsqrt(variance + 1e-05) * norm_gain + norm_bias).astype(jnp.bfloat16)


def row_codes(routes, gate_codes, owners, capacity):
    rows = routes.shape[0]
    match = routes[:, :, None] == jnp.arange(owners, dtype=jnp.int32)[None, None, :]
    codes = jnp.sum(jnp.where(match, gate_codes[:, :, None], 0), axis=1).astype(jnp.float32)
    named = jnp.any(match, axis=1)
    before = lax.broadcasted_iota(jnp.int32, (rows, rows), 1) < lax.broadcasted_iota(
        jnp.int32, (rows, rows), 0
    )
    named_b = named.astype(jnp.bfloat16)
    rank = jnp.dot(before.astype(jnp.bfloat16), named_b, preferred_element_type=jnp.float32)
    hot = jnp.argmax(jnp.sum(named.astype(jnp.float32), axis=0))
    kept = (rank < capacity) | (jnp.arange(owners)[None, :] == hot)
    return jnp.where(kept, codes, 0.0)


LANES = 128
STEP = 16


def fused(
    owners, top, capacity, tokens, gain, bias, routes, gates, w_in_hbm, w_out_hbm, base_out, from_x, from_y,
    rows_all, codes, part, sib, diag_in, base, hid, weight, w_in, w_up, w_out,
    load_sem, send_sem, recv_sem,
):
    n = tokens.shape[0]
    half = n // 2
    width = tokens.shape[1]
    inner = w_out.shape[0]
    me = lax.axis_index("exp")
    core, across, along = me % 2, me // 2 % 2, me // 4

    def peer(rel):
        c = 1 - core if rel % 2 else core
        x = 1 - across if rel // 2 % 2 else across
        y = 1 - along if rel // 4 else along
        return {"exp": y * 4 + x * 2 + c}

    sibling, x_near, y_near = 1, 2, 4

    def move(index, src, dst, rel):
        return pltpu.make_async_remote_copy(
            src_ref=src,
            dst_ref=dst,
            send_sem=send_sem.at[index],
            recv_sem=recv_sem.at[index],
            device_id=peer(rel),
            device_id_type=pl.DeviceIdType.MESH,
        )

    first, second = pl.ds(0, n), pl.ds(n, n)
    upper, lower = pl.ds(0, half), pl.ds(half, half)
    load_in = pltpu.make_async_copy(w_in_hbm.at[0], w_in, load_sem.at[0])
    load_out = pltpu.make_async_copy(w_out_hbm.at[0], w_out, load_sem.at[1])
    load_in.start()
    load_out.start()
    barrier = pltpu.get_barrier_semaphore()
    for rel in range(1, 8):
        pl.semaphore_signal(
            barrier, inc=1, device_id=peer(rel), device_id_type=pl.DeviceIdType.MESH
        )

    @pl.loop(0, n // STEP)
    def _(i):
        at = pl.ds(pl.multiple_of(i * STEP, STEP), STEP)
        values = tokens[at, :].astype(jnp.float32)
        average = jnp.mean(values, axis=1, keepdims=True)
        centered = values - average
        variance = jnp.mean(centered * centered, axis=1, keepdims=True)
        scaled = centered * lax.rsqrt(variance + 1e-05) * gain[...] + bias[...]
        rows_all[0, at, :] = scaled.astype(jnp.bfloat16)

    pl.semaphore_wait(barrier, 7)
    a_x = move(0, rows_all.at[0, upper], rows_all.at[1, upper], x_near)
    b_y = move(1, rows_all.at[0, lower], rows_all.at[1, lower], y_near)
    to_sib = move(2, rows_all.at[0, first], rows_all.at[0, second], sibling)
    a_x.start()
    b_y.start()
    to_sib.start()

    expert_row = lax.broadcasted_iota(jnp.int32, (owners, n), 0)
    code = jnp.zeros((owners, n), jnp.int32)
    named = jnp.zeros((owners, n), jnp.float32)
    for j in range(top):
        match = routes[j : j + 1, :] == expert_row
        code = code + jnp.where(match, gates[j : j + 1, :], 0)
        named = named + jnp.where(match, 1.0, 0.0)
    before = jnp.where(
        lax.broadcasted_iota(jnp.int32, (n, n), 0) < lax.broadcasted_iota(jnp.int32, (n, n), 1),
        1.0,
        0.0,
    ).astype(jnp.bfloat16)
    rank = jnp.dot(named.astype(jnp.bfloat16), before, preferred_element_type=jnp.float32)
    counts = jnp.sum(named, axis=1, keepdims=True)
    most = jnp.max(counts, axis=0, keepdims=True)
    index = expert_row.astype(jnp.float32)
    hot = jnp.min(jnp.where(counts == most, index, 1e9), axis=0, keepdims=True)
    code = jnp.where((rank < capacity) | (index == hot), code, 0)
    low = code % 4
    both = jnp.concatenate([code - low, low], axis=0).astype(jnp.float32)
    codes[0] = jnp.zeros(codes.shape[1:], jnp.bfloat16)
    codes[0, :, 0:n] = both.astype(jnp.bfloat16)
    code_moves = [None] + [move(7 + rel, codes.at[0], codes.at[rel], rel) for rel in range(1, 8)]
    for rel in range(1, 8):
        code_moves[rel].start()

    row16 = lax.broadcasted_iota(jnp.int32, (2 * owners, LANES), 0)
    choose = jnp.where((row16 == me) | (row16 == me + owners), 1.0, 0.0).astype(jnp.bfloat16)

    up_width = w_up.shape[1]

    def expert(k):
        if k == 0:
            pieces = ((0, 0, 0, n), (n, 1, 0, n))
        elif k == 2:
            pieces = ((0, 6, 0, n), (n, 7, 0, n))
        else:
            x_from, y_from = (0, half) if k == 1 else (half, 0)
            pieces = (
                (0, 2, x_from, half), (half, 4, y_from, half),
                (n, 3, x_from, half), (n + half, 5, y_from, half),
            )
        for at, slot, start, count in pieces:
            column = lax.dot_general(
                codes[slot],
                choose,
                (((0,), (0,)), ((), ())),
                preferred_element_type=jnp.float32,
            )
            weight[at : at + count, :] = column[start : start + count, :] * (1.0 / 1024.0)

        @pl.loop(0, up_width // 256)
        def _(i):
            at = pl.ds(pl.multiple_of(i * 256, 256), 256)
            a = jnp.dot(rows_all[k], w_in[:, at], preferred_element_type=jnp.float32)
            b = jnp.dot(rows_all[k], w_up[:, at], preferred_element_type=jnp.float32)
            hid[:, at] = (a / (1.0 + jnp.exp(-a)) * b).astype(jnp.bfloat16)

        @pl.loop(0, width // 256)
        def _(i):
            at = pl.ds(pl.multiple_of(i * 256, 256), 256)
            y = jnp.dot(hid[:, :inner], w_out[:, at], preferred_element_type=jnp.float32)
            scale = weight[...]
            part[k, :, at] = (y * jnp.concatenate([scale, scale], axis=1)).astype(jnp.bfloat16)

    def add(dst, terms, count):
        @pl.loop(0, count // STEP)
        def _(i):
            at = pl.ds(pl.multiple_of(i * STEP, STEP), STEP)
            total = terms[0][at, :].astype(jnp.float32)
            for term in terms[1:]:
                total = total + term[at, :].astype(jnp.float32)
            dst[at, :] = total.astype(dst.dtype)

    part_moves = [move(3 + k, part.at[k, second], sib.at[k], sibling) for k in range(4)]
    row_sib = [None] + [
        move(14 + k, rows_all.at[k, first], rows_all.at[k, second], sibling) for k in range(1, 4)
    ]
    x_on = move(18, rows_all.at[1, upper], rows_all.at[2, upper], y_near)
    y_on = move(19, rows_all.at[1, lower], rows_all.at[2, lower], x_near)
    b_x = move(20, rows_all.at[0, lower], rows_all.at[3, upper], x_near)
    a_y = move(21, rows_all.at[0, upper], rows_all.at[3, lower], y_near)
    sum_a_x = move(22, part.at[1, upper], from_x.at[upper], x_near)
    sum_b_y = move(23, part.at[1, lower], from_y.at[lower], y_near)
    sum_d_x = move(24, part.at[2, upper], diag_in.at[upper], x_near)
    sum_d_y = move(25, part.at[2, lower], diag_in.at[lower], y_near)
    sum_b_x = move(26, part.at[3, upper], from_x.at[lower], x_near)
    sum_a_y = move(27, part.at[3, lower], from_y.at[upper], y_near)

    b_x.start()
    a_y.start()

    load_in.wait()

    @pl.loop(0, width // STEP)
    def _(i):
        at = pl.ds(pl.multiple_of(i * STEP, STEP), STEP)
        turned_in = pltpu.roll(w_in[at, :].astype(jnp.float32), inner, 1)
        w_up[at, :] = turned_in[:, :up_width].astype(jnp.bfloat16)

    load_out.wait()
    to_sib.wait_recv()
    code_moves[1].wait_recv()
    expert(0)
    part_moves[0].start()
    a_x.wait_recv()
    x_on.start()
    b_y.wait_recv()
    y_on.start()
    row_sib[1].start()
    for rel in range(2, 8):
        code_moves[rel].wait_recv()
    part_moves[0].wait_recv()
    add(base, [part.at[0, first], sib.at[0]], n)
    base_move = pltpu.make_async_copy(base, base_out, load_sem.at[2])
    base_move.start()
    row_sib[1].wait_recv()
    expert(1)
    part_moves[1].start()
    part_moves[1].wait_recv()
    mine = part.at[1, first]
    add(mine, [mine, sib.at[1]], n)
    sum_a_x.start()
    sum_b_y.start()
    x_on.wait_recv()
    y_on.wait_recv()
    row_sib[2].start()
    row_sib[2].wait_recv()
    expert(2)
    part_moves[2].start()
    part_moves[2].wait_recv()
    mine = part.at[2, first]
    add(mine, [mine, sib.at[2]], n)
    sum_d_x.start()
    sum_d_y.start()
    b_x.wait_recv()
    a_y.wait_recv()
    row_sib[3].start()
    row_sib[3].wait_recv()
    expert(3)
    part_moves[3].start()
    part_moves[3].wait_recv()
    sum_d_x.wait_recv()
    mine = part.at[3, lower]
    add(mine, [mine, sib.at[3, lower], diag_in.at[upper]], half)
    sum_a_y.start()
    sum_d_y.wait_recv()
    mine = part.at[3, upper]
    add(mine, [mine, sib.at[3, upper], diag_in.at[lower]], half)
    sum_b_x.start()
    sum_a_x.wait_recv()
    sum_b_y.wait_recv()
    sum_a_y.wait_recv()
    sum_b_x.wait_recv()
    base_move.wait()
    for sent in (
        [a_x, b_y, to_sib, x_on, y_on, b_x, a_y]
        + row_sib[1:]
        + code_moves[1:]
        + part_moves
        + [sum_a_x, sum_b_y, sum_d_x, sum_d_y, sum_b_x, sum_a_y]
    ):
        sent.wait_send()


def fused_call(tokens, norm_gain, norm_bias, routes, gate_codes, w_in, w_out, capacity):
    owners = lax.axis_size("exp")
    n, width = tokens.shape
    inner = w_out.shape[1]
    top = routes.shape[1]
    wide = -(-inner // 256) * 256
    vmem = pl.BlockSpec(memory_space=pltpu.VMEM)
    anywhere = pl.BlockSpec(memory_space=pl.ANY)
    bf16, f32 = jnp.bfloat16, jnp.float32

    def body(*refs):
        fused(owners, top, capacity, *refs)

    flops = 2 * owners * n * width * inner * 3
    base, from_x, from_y = pl.pallas_call(
        body,
        out_shape=[jax.ShapeDtypeStruct((n, width), kind) for kind in (f32, bf16, bf16)],
        in_specs=[vmem] * 5 + [anywhere] * 2,
        out_specs=[anywhere] * 3,
        scratch_shapes=[
            pltpu.VMEM((4, 2 * n, width), bf16),
            pltpu.VMEM((8, 2 * owners, -(-n // LANES) * LANES), bf16),
            pltpu.VMEM((4, 2 * n, width), bf16),
            pltpu.VMEM((4, n, width), bf16),
            pltpu.VMEM((n, width), bf16),
            pltpu.VMEM((n, width), f32),
            pltpu.VMEM((2 * n, wide), bf16),
            pltpu.VMEM((2 * n, LANES), f32),
            pltpu.VMEM((width, 2 * inner), bf16),
            pltpu.VMEM((width, wide), bf16),
            pltpu.VMEM((inner, width), bf16),
            pltpu.SemaphoreType.DMA((3,)),
            pltpu.SemaphoreType.DMA((28,)),
            pltpu.SemaphoreType.DMA((28,)),
        ],
        compiler_params=pltpu.CompilerParams(
            collective_id=0, has_side_effects=True, vmem_limit_bytes=56 * 2**20
        ),
        cost_estimate=pl.CostEstimate(
            flops=flops, bytes_accessed=6 * width * inner, transcendentals=owners * n * inner
        ),
    )(tokens, norm_gain[None, :], norm_bias[None, :], routes.T, gate_codes.T, w_in, w_out)
    return (base + from_x.astype(f32) + from_y.astype(f32)).astype(bf16)


def local(tokens, norm_gain, norm_bias, routes, gate_codes, w_in, w_out):
    owners = lax.axis_size("exp")
    rows = tokens.shape[0]
    capacity = min(rows, rows * routes.shape[1] * 9 // (8 * owners))
    if owners == 8:
        return fused_call(
            tokens, norm_gain, norm_bias, routes, gate_codes, w_in, w_out, capacity
        )
    normed = layer_norm(tokens, norm_gain, norm_bias)
    codes = row_codes(routes, gate_codes, owners, capacity)
    all_rows = lax.all_gather(normed, "exp", axis=0, tiled=True)
    all_codes = lax.all_gather(codes, "exp", axis=0, tiled=True)
    me = lax.axis_index("exp")
    weight = lax.dynamic_slice_in_dim(all_codes, me, 1, 1) * (1.0 / 1024.0)
    inner = w_out.shape[1]
    projected = jnp.dot(all_rows, w_in[0], preferred_element_type=jnp.float32)
    hidden = (jax.nn.silu(projected[:, :inner]) * projected[:, inner:]).astype(jnp.bfloat16)
    results = jnp.dot(hidden, w_out[0], preferred_element_type=jnp.float32)
    part = (results * weight).astype(jnp.bfloat16)
    return lax.psum_scatter(part, "exp", scatter_dimension=0, tiled=True)


def solution(mesh):
    return jax.shard_map(
        local,
        mesh=mesh,
        in_specs=(
            P(("seq", "exp"), None),
            P(),
            P(),
            P(("seq", "exp"), None),
            P(("seq", "exp"), None),
            P("exp", None, None),
            P("exp", None, None),
        ),
        out_specs=P(("seq", "exp"), None),
        check_vma=False,
    )
```
